128 devices in a mesh: rng: 16 (over z_lo, x, core), az: 8 (over z_hi, y).
Axes of the slice: x: 4, y: 4, z: 4 (z_hi: 2, z_lo: 2; z = z_hi * 2 + z_lo), core: 2. Of those that a mesh axis runs over, the one named last changes fastest.
Arguments:
- residual: float32 [2, 2, 2048, 16384], P(None, None, 'az', 'rng'), may hold values from -45 to 45
- range_chirp: float32 [2, 256], replicated, may hold values from -0.25 to 0.25
- az_kernel: float32 [128, 2, 1024], P(('rng', 'az')), may hold values from -0.125 to 0.125
- image_now: float32 [2, 2, 2048, 16384], P(None, None, None, ('rng', 'az')), may hold values from -6 to 6
Outputs:
- image_next: float32 [2, 2, 2048, 16384], P(None, None, None, ('rng', 'az'))
- root_mean: float32 [], replicated
The draws below stay inside these ranges and needn't reach their ends.
All inputs are finite; a program needn't handle non-finite values.
Results may differ from the reference program's by a relative error of at most 0.000051.
Values sent between devices are 32-bit elements; how exact they have to be, the bound alone decides.
A program may use at most 128 MiB of HBM per device.

```python
import jax
import jax.numpy as jnp
from jax import lax

POL = 2
KR = 256
KA = 1024
NA = 2048
NR = 16384
RB = 128
RANGE_BLOCKS = 128


def draw_residual(key, part):
    shape = (POL, 2, NA, NR)
    az_pos = lax.broadcasted_iota(jnp.float32, shape, 2) / NA
    rng_pos = lax.broadcasted_iota(jnp.float32, shape, 3) / NR
    noise = jnp.clip(jax.random.normal(key, shape, jnp.float32), -6.0, 6.0)
    scale = (1.0 + 2.0 * rng_pos) * (1.0 + 1.5 * az_pos)
    return scale * noise


def levels(key, dims, shards, least, top_value):
    loudness, own = 1.0, jax.random.fold_in(key, 6)
    for axis_at, blocks in shards:
        heights = jnp.exp(jax.random.uniform(jax.random.fold_in(own, axis_at), (blocks,), jnp.float32, least / len(shards), top_value / len(shards)))
        loudness = loudness * jnp.repeat(heights, dims[axis_at] // blocks).reshape([-1 if axis == axis_at else 1 for axis in range(len(dims))])
    return loudness


def centred(own_key, extent, scale, limit, shards=(), kind=jnp.bfloat16):
    array = scale * jax.random.normal(own_key, extent, jnp.float32)
    if shards:
        array = array * levels(own_key, extent, shards, -0.22, 0.18)
    return jnp.clip(array, -limit, limit).astype(kind)


def setup_inputs(seed: int = 0) -> dict:
    streams_of = jax.random.split(jax.random.key(seed), 5)
    return {
        "residual": draw_residual(jax.random.fold_in(streams_of[4], 71), 0),
        "range_chirp": centred(streams_of[1], (2, KR), (2 * KR) ** -0.5, 0.25, (), jnp.float32),
        "az_kernel": centred(streams_of[2], (RANGE_BLOCKS, 2, KA), (2 * KA) ** -0.5, 0.125, ((0, 128),), jnp.float32),
        "image_now": centred(streams_of[3], (POL, 2, NA, NR), 1.0, 6.0, ((3, 128),), jnp.float32),
    }


step_size = 0.5
reg_weight = 0.25
epsilon = 1e-06

def toeplitz_rows(taps_vec, row_count, col_count):
    padded = jnp.concatenate([taps_vec, jnp.zeros((col_count + 1 - taps_vec.shape[0],), taps_vec.dtype)])
    flattened = jnp.tile(padded, row_count)[:row_count * col_count]
    return flattened.reshape(row_count, col_count)

def range_correlate(padded, range_chirp, tile_cols):
    tap_count = range_chirp.shape[1]
    span_cols = padded.shape[3] - tap_count
    tile_count = span_cols // tile_cols
    shifts = tap_count // tile_cols + 1
    length = tile_cols * shifts
    blocks = padded.reshape(padded.shape[0], 2, padded.shape[2], tile_count + shifts - 1, tile_cols)
    windows = jnp.concatenate([blocks[:, :, :, offset:offset + tile_count] for offset in range(shifts)], axis=4)
    real_part = toeplitz_rows(range_chirp[0], tile_cols, length).T
    imag_part = toeplitz_rows(range_chirp[1], tile_cols, length).T
    matrix = jnp.stack([jnp.stack([real_part, -imag_part], 1), jnp.stack([imag_part, real_part], 1)], 0)
    result = jnp.einsum('pqatm,qmoj->poatj', windows, matrix, precision=lax.Precision.HIGHEST)
    return result.reshape(padded.shape[0], 2, padded.shape[2], span_cols)

def azimuth_correlate(turned, kernel_pair):
    tap_count = kernel_pair.shape[1]
    tile_rows = tap_count // 2
    tile_count = turned.shape[2] // tile_rows
    padded = jnp.pad(turned, ((0, 0), (0, 0), (tile_rows, tile_rows), (0, 0)))
    blocks = padded.reshape(turned.shape[0], 2, tile_count + 2, tile_rows, turned.shape[3])
    windows = jnp.concatenate([blocks[:, :, offset:offset + tile_count] for offset in range(3)], axis=3)
    real_part = toeplitz_rows(kernel_pair[0], tile_rows, 3 * tile_rows)
    imag_part = toeplitz_rows(kernel_pair[1], tile_rows, 3 * tile_rows)
    matrix = jnp.stack([jnp.stack([real_part, imag_part], 1), jnp.stack([-imag_part, real_part], 1)], 0)
    result = jnp.einsum('oiqm,pqtmw->potiw', matrix, windows, precision=lax.Precision.HIGHEST)
    return result.reshape(turned.shape)

def laplacian(image_now, range_padded):
    az_padded = jnp.pad(image_now, ((0, 0), (0, 0), (1, 1), (0, 0)))
    result = 4.0 * image_now - az_padded[:, :, 2:, :] - az_padded[:, :, :-2, :]
    return result - range_padded[:, :, :, 2:] - range_padded[:, :, :, :-2]

def reference(residual, range_chirp, az_kernel, image_now):
    grand_total = jnp.sum(residual * residual)
    root_mean = jnp.sqrt(grand_total / (2.0 * NA * NR) + epsilon)
    half_taps = KR // 2
    padded = jnp.pad(residual, ((0, 0), (0, 0), (0, 0), (half_taps, half_taps)))

    def one_channel(channel):
        return range_correlate(channel[None], range_chirp, KR)[0]
    ranged = lax.map(one_channel, padded)
    blocks = ranged.reshape(POL, 2, NA, RANGE_BLOCKS, RB).transpose(3, 0, 1, 2, 4)

    def one_block(inputs):
        return azimuth_correlate(inputs[0], inputs[1])
    turned = lax.map(one_block, (blocks, az_kernel))
    adjoint = turned.transpose(1, 2, 3, 0, 4).reshape(POL, 2, NA, NR)
    range_padded = jnp.pad(image_now, ((0, 0), (0, 0), (0, 0), (1, 1)))
    image_next = image_now - step_size * (adjoint / root_mean + reg_weight * laplacian(image_now, range_padded))
    return (image_next, root_mean)
```

```python
import jax
import jax.numpy as jnp
from jax import lax
from jax.experimental import pallas as pl
from jax.experimental.pallas import tpu as pltpu
from jax.sharding import PartitionSpec as P

step_size = 0.5
reg_weight = 0.25
epsilon = 1e-06

F32 = jnp.float32
BF16 = jnp.bfloat16
MESH = pl.DeviceIdType.MESH
GROUP = 8
OTHERS = GROUP - 1
TURN = ((0, 1), (1, 0), (2, 1), (3, 0), (1, 1), (2, 0), (3, 1))
STAGES = 7


def dot(a, b):
    return jnp.dot(a, b, preferred_element_type=F32)


def split(value):
    high = value.astype(BF16)
    return high, (value - high.astype(F32)).astype(BF16)


def toeplitz(row, rows):
    wide = jnp.broadcast_to(row, (rows, row.shape[1]))
    return pltpu.roll(wide, 0, 1, stride=1, stride_axis=0)


def kernel(
    res, chirp, azk, img,
    out, rm_out,
    xf, xh, xl, ch, cl, lh, ll, sb, rv, yh, yl, acc, im, base, pk, pc, sm,
    ld, hs, hr, ss, rs, es, er, cs, cr, os,
):
    rng, az = lax.axis_index("rng"), lax.axis_index("az")
    zh, y = az // 4, az % 4
    flat = rng * 8 + az
    to_az = [((zh + dz) % 2) * 4 + (y + dy) % 4 for dy, dz in TURN]
    from_az = [((zh + dz) % 2) * 4 + (y + 4 - dy) % 4 for dy, dz in TURN]
    rng_next, rng_prev = (rng + 1) % 16, (rng + 15) % 16
    col_next, col_prev = (flat + 1) % 128, (flat + 127) % 128

    def partner(stage):
        width = 2**stage
        other = flat + (1 - 2 * ((flat // width) % 2)) * width
        return (other // 8, other % 8)

    load_img = pltpu.make_async_copy(img, im.at[:, :, pl.ds(8, 2048)], ld.at[8])

    def load_block(b):
        return pltpu.make_async_copy(
            res.at[:, :, :, pl.ds(128 * b, 128)], xf.at[b + 1], ld.at[b]
        )

    for b in range(8):
        load_block(b).start()
    load_img.start()

    barrier = pltpu.get_barrier_semaphore()
    peers = [(rng, to_az[t]) for t in range(OTHERS)]
    peers += [(rng_next, az), (rng_prev, az)]
    peers += [(col_next // 8, col_next % 8), (col_prev // 8, col_prev % 8)]
    peers += [partner(stage) for stage in range(STAGES)]
    for peer in peers:
        pl.semaphore_signal(barrier, inc=1, device_id=peer, device_id_type=MESH)

    lanes = jnp.zeros((1, 128), F32)
    cr_t = toeplitz(jnp.concatenate([chirp[0:1, :], lanes], 1), 128).T
    ci_t = toeplitz(jnp.concatenate([chirp[1:2, :], lanes], 1), 128).T
    for rows, left, right in ((0, cr_t, -ci_t), (384, ci_t, cr_t)):
        for cols, part in ((0, left), (128, right)):
            high, low = split(part)
            ch[rows : rows + 384, cols : cols + 128] = high
            cl[rows : rows + 384, cols : cols + 128] = low

    pl.semaphore_wait(barrier, len(peers))

    to_next = pltpu.make_async_remote_copy(
        src_ref=res.at[:, :, :, pl.ds(896, 128)], dst_ref=xf.at[0],
        send_sem=hs.at[0], recv_sem=hr.at[0],
        device_id=(rng_next, az), device_id_type=MESH,
    )
    to_prev = pltpu.make_async_remote_copy(
        src_ref=res.at[:, :, :, pl.ds(0, 128)], dst_ref=xf.at[9],
        send_sem=hs.at[1], recv_sem=hr.at[1],
        device_id=(rng_prev, az), device_id_type=MESH,
    )

    @pl.when(rng < 15)
    def _():
        to_next.start()

    @pl.when(rng > 0)
    def _():
        to_prev.start()

    def split_block(b):
        for p in range(2):
            for c in range(2):
                high, low = split(xf[b, p, c])
                xh[b, c, p * 256 : (p + 1) * 256] = high
                xl[b, c, p * 256 : (p + 1) * 256] = low

    sm[0] = jnp.zeros((8, 128), F32)
    for b in range(8):
        load_block(b).wait()

    def first(b, carry):
        split_block(b)
        total = sm[0]
        for p in range(2):
            for c in range(2):
                v = xf[b, p, c]
                total += jnp.sum((v * v).reshape(32, 8, 128), axis=0)
        sm[0] = total
        return carry

    lax.fori_loop(1, 9, first, 0)

    def range_block(j, slot):
        high = jnp.concatenate([xh[j + q, c] for c in range(2) for q in range(3)], 1)
        low = jnp.concatenate([xl[j + q, c] for c in range(2) for q in range(3)], 1)
        result = dot(high, ch[...]) + dot(low, ch[...]) + dot(high, cl[...])
        for p in range(2):
            for c in range(2):
                sb[slot, c * 256 : (c + 1) * 256, p * 128 : (p + 1) * 128] = result[
                    p * 256 : (p + 1) * 256, c * 128 : (c + 1) * 128
                ]

    def turn_copy(t):
        dz, dy = 1 - t % 2, t - 3 * (t // 4)
        target = ((zh + dz) % 2) * 4 + (y + dy) % 4
        return target, pltpu.make_async_remote_copy(
            src_ref=sb.at[t], dst_ref=rv.at[t], send_sem=ss.at[t], recv_sem=rs.at[t],
            device_id=(rng, target), device_id_type=MESH,
        )

    def inner(j):
        return jnp.logical_and(j > 0, j < 7)

    def send_inner(t, carry):
        target, copy = turn_copy(t)

        @pl.when(inner(target))
        def _():
            range_block(target, t)
            copy.start()

        return carry

    lax.fori_loop(0, OTHERS, send_inner, 0)

    lanes = jnp.zeros((1, 256), F32)
    wr = toeplitz(jnp.concatenate([azk[0, 0:1, :], lanes], 1), 256)
    wi = toeplitz(jnp.concatenate([azk[0, 1:2, :], lanes], 1), 256)
    for e in range(5):
        part_r, part_i = wr[:, 256 * e : 256 * e + 256], wi[:, 256 * e : 256 * e + 256]
        for rows, left, right in ((0, part_r, part_i), (256, -part_i, part_r)):
            for cols, part in ((0, left), (256, right)):
                high, low = split(part)
                lh[e, rows : rows + 256, cols : cols + 256] = high
                ll[e, rows : rows + 256, cols : cols + 256] = low

    @pl.when(rng > 0)
    def _():
        to_next.wait_recv()

    @pl.when(rng == 0)
    def _():
        xf[0] = jnp.zeros_like(xf[0])

    @pl.when(rng < 15)
    def _():
        to_prev.wait_recv()

    @pl.when(rng == 15)
    def _():
        xf[9] = jnp.zeros_like(xf[9])

    split_block(0)
    split_block(9)

    def send_outer(t, carry):
        target, copy = turn_copy(t)

        @pl.when(jnp.logical_not(inner(target)))
        def _():
            range_block(target, t)
            copy.start()

        return carry

    lax.fori_loop(0, OTHERS, send_outer, 0)
    range_block(az, OTHERS)

    load_img.wait()
    for p in range(2):
        for c in range(2):
            im[p, c, 0:8] = jnp.zeros((8, 128), F32)
            im[p, c, 2056:2064] = jnp.zeros((8, 128), F32)

    def pack(k, carry):
        at = pl.multiple_of(128 * k, 128)
        for p in range(2):
            for c in range(2):
                turned = im[p, c, pl.ds(at + 8, 128), :].T
                row = 2 * p + c
                pk[row : row + 1, pl.ds(at, 128)] = turned[0:1]
                pk[row + 4 : row + 5, pl.ds(at, 128)] = turned[127:128]
        return carry

    lax.fori_loop(0, 16, pack, 0)

    def column_copy(side, target):
        return pltpu.make_async_remote_copy(
            src_ref=pk, dst_ref=pc.at[side], send_sem=cs.at[side], recv_sem=cr.at[side],
            device_id=(target // 8, target % 8), device_id_type=MESH,
        )

    cols = [column_copy(0, col_next), column_copy(1, col_prev)]
    for copy in cols:
        copy.start()

    acc[...] = jnp.zeros_like(acc)

    def azimuth(source, s):
        high, low = split(source)
        yh[...] = high
        yl[...] = low

        def tile(e, carry):
            i = s + 2 - e

            @pl.when(jnp.logical_and(i >= 0, i < 8))
            def _():
                acc[i] += dot(lh[e], yh[...]) + dot(lh[e], yl[...]) + dot(ll[e], yh[...])

            return carry

        lax.fori_loop(0, 5, tile, 0)

    def sum_copy(stage):
        return pltpu.make_async_remote_copy(
            src_ref=sm.at[2 * stage], dst_ref=sm.at[2 * stage + 1],
            send_sem=es.at[stage], recv_sem=er.at[stage],
            device_id=partner(stage), device_id_type=MESH,
        )

    def regularize():
        for copy in cols:
            copy.wait_recv()
        lane = lax.broadcasted_iota(jnp.int32, (128, 128), 1)
        has_prev = jnp.where(flat > 0, 1.0, 0.0)
        has_next = jnp.where(flat < 127, 1.0, 0.0)

        def rows(k, carry):
            at = pl.multiple_of(128 * k, 128)
            before = pc[0, :, pl.ds(at, 128)].T * has_prev
            after = pc[1, :, pl.ds(at, 128)].T * has_next
            for p in range(2):
                for c in range(2):
                    row = 2 * p + c
                    v = im[p, c, pl.ds(at, 144), :]
                    mid = v[8:136]
                    left = jnp.where(lane == 0, before[:, row + 4 : row + 5], pltpu.roll(mid, 1, 1))
                    right = jnp.where(lane == 127, after[:, row : row + 1], pltpu.roll(mid, 127, 1))
                    lap = 4.0 * mid - v[9:137] - v[7:135] - right - left
                    base[p, c, pl.ds(at, 128), :] = mid - (step_size * reg_weight) * lap
            return carry

        lax.fori_loop(0, 16, rows, 0)

    for n in range(8):
        if n < STAGES:
            sum_copy(n).start()
        if n == 0:
            azimuth(sb[OTHERS], az)
        else:
            turn_copy(n - 1)[1].wait_recv()
            azimuth(rv[n - 1], from_az[n - 1])
        if n < STAGES:
            sum_copy(n).wait()
            sm[2 * n + 2] = sm[2 * n] + sm[2 * n + 1]
        if n == 1:
            regularize()

    entries = 2.0 * 2048 * 16384
    total = jnp.sum(sm[2 * STAGES], axis=(0, 1), keepdims=True)
    root_mean = jnp.sqrt(total / entries + epsilon)
    rm_out[...] = root_mean
    scale = step_size / root_mean

    def out_copy(i):
        lines = pl.ds(pl.multiple_of(256 * i, 256), 256)
        return pltpu.make_async_copy(base.at[:, :, lines], out.at[:, :, lines], os.at[i])

    def finish(i, carry):
        at = pl.multiple_of(256 * i, 256)
        for p in range(2):
            for c in range(2):
                base[p, c, pl.ds(at, 256), :] = (
                    base[p, c, pl.ds(at, 256), :]
                    - acc[i, c * 256 : (c + 1) * 256, p * 128 : (p + 1) * 128] * scale
                )
        out_copy(i).start()
        return carry

    lax.fori_loop(0, 8, finish, 0)

    for i in range(8):
        out_copy(i).wait()
    for t in range(OTHERS):
        turn_copy(t)[1].wait_send()
    for copy in cols:
        copy.wait_send()

    @pl.when(rng < 15)
    def _():
        to_next.wait_send()

    @pl.when(rng > 0)
    def _():
        to_prev.wait_send()


def local(residual, range_chirp, az_kernel, image_now):
    vmem = pl.BlockSpec(memory_space=pltpu.VMEM)
    anywhere = pl.BlockSpec(memory_space=pl.ANY)
    dma = pltpu.SemaphoreType.DMA
    image_next, root_mean = pl.pallas_call(
        kernel,
        out_shape=(
            jax.ShapeDtypeStruct(image_now.shape, F32),
            jax.ShapeDtypeStruct((1, 1), F32),
        ),
        in_specs=[anywhere, vmem, vmem, anywhere],
        out_specs=(anywhere, vmem),
        scratch_shapes=[
            pltpu.VMEM((10, 2, 2, 256, 128), F32),
            pltpu.VMEM((10, 2, 512, 128), BF16),
            pltpu.VMEM((10, 2, 512, 128), BF16),
            pltpu.VMEM((768, 256), BF16),
            pltpu.VMEM((768, 256), BF16),
            pltpu.VMEM((5, 512, 512), BF16),
            pltpu.VMEM((5, 512, 512), BF16),
            pltpu.VMEM((8, 512, 256), F32),
            pltpu.VMEM((7, 512, 256), F32),
            pltpu.VMEM((512, 256), BF16),
            pltpu.VMEM((512, 256), BF16),
            pltpu.VMEM((8, 512, 256), F32),
            pltpu.VMEM((2, 2, 2064, 128), F32),
            pltpu.VMEM((2, 2, 2048, 128), F32),
            pltpu.VMEM((8, 2048), F32),
            pltpu.VMEM((2, 8, 2048), F32),
            pltpu.VMEM((2 * STAGES + 1, 8, 128), F32),
            dma((9,)), dma((2,)), dma((2,)), dma((7,)), dma((7,)),
            dma((STAGES,)), dma((STAGES,)), dma((2,)), dma((2,)), dma((8,)),
        ],
        compiler_params=pltpu.CompilerParams(
            collective_id=0, has_side_effects=True, vmem_limit_bytes=50 << 20
        ),
        cost_estimate=pl.CostEstimate(
            flops=20_000_000_000, bytes_accessed=12 << 20, transcendentals=0
        ),
        name="sar_step",
    )(residual, range_chirp, az_kernel, image_now)
    return image_next, root_mean.reshape(())


def solution(mesh):
    placed = (
        P(None, None, "az", "rng"),
        P(),
        P(("rng", "az"), None, None),
        P(None, None, None, ("rng", "az")),
    )
    return jax.shard_map(
        local,
        mesh=mesh,
        in_specs=placed,
        out_specs=(P(None, None, None, ("rng", "az")), P()),
        check_vma=False,
    )
```

```python
import jax
import jax.numpy as jnp
from jax import lax
from jax.experimental import pallas as pl
from jax.experimental.pallas import tpu as pltpu
from jax.sharding import PartitionSpec as P

step_size = 0.5
reg_weight = 0.25
epsilon = 1e-06

F32 = jnp.float32
BF16 = jnp.bfloat16
MESH = pl.DeviceIdType.MESH
GROUP = 8
OTHERS = GROUP - 1
COLS = 16
PARTS = 2
UNIT = 128
TURN = ((0, 1), (1, 0), (2, 1), (3, 0), (1, 1), (2, 0), (3, 1))


def dot(a, b):
    return jnp.dot(a, b, preferred_element_type=F32)


def split(value):
    high = value.astype(BF16)
    return high, (value - high.astype(F32)).astype(BF16)


def toeplitz(row, rows):
    wide = jnp.broadcast_to(row, (rows, row.shape[1]))
    return pltpu.roll(wide, 0, 1, stride=1, stride_axis=0)


def kernel(
    res, chirp, azk, img,
    out, rm_out,
    xf, xh, xl, cv, av, ch, cl, az_mat, sb, rv, x3, im, pk, pc, sm,
    ld, hs, hr, ss, rs, ps, pr, qs, qr, cs, cr,
):
    rng, az = lax.axis_index("rng"), lax.axis_index("az")
    zh, y = az // 4, az % 4
    flat = rng * 8 + az
    to_az = [((zh + dz) % 2) * 4 + (y + dy) % 4 for dy, dz in TURN]
    to_rng = [(rng + k) % COLS for k in range(1, COLS)]
    rng_next, rng_prev = (rng + 1) % 16, (rng + 15) % 16
    col_next, col_prev = (flat + 1) % 128, (flat + 127) % 128

    def load_block(b):
        return pltpu.make_async_copy(
            res.at[:, :, :, pl.ds(128 * b, 128)], xf.at[b + 1], ld.at[b]
        )

    load_chirp = pltpu.make_async_copy(chirp, cv, ld.at[8])
    load_azk = pltpu.make_async_copy(azk.at[0], av, ld.at[9])
    load_img = [
        pltpu.make_async_copy(img.at[q // 2, q % 2], im.at[q, pl.ds(8, 2048)], ld.at[10 + q])
        for q in range(4)
    ]
    for b in range(8):
        load_block(b).start()
    load_chirp.start()
    load_azk.start()
    for copy in load_img:
        copy.start()

    barrier = pltpu.get_barrier_semaphore()
    peers = [(rng, target) for target in to_az]
    peers += [(target, az) for target in to_rng]
    peers += [(col_next // 8, col_next % 8), (col_prev // 8, col_prev % 8)]
    for peer in peers:
        pl.semaphore_signal(barrier, inc=1, device_id=peer, device_id_type=MESH)

    for b in range(8):
        load_block(b).wait()

    def squares(b, total):
        for p in range(2):
            for c in range(2):
                v = xf[b, p, c]
                total += jnp.sum((v * v).reshape(32, 8, 128), axis=0)
        return total

    sm[az] = lax.fori_loop(1, 9, squares, jnp.zeros((8, 128), F32))

    pl.semaphore_wait(barrier, len(peers))

    def halo_copy(side, h):
        lines = pl.ds(UNIT * h, UNIT)
        return pltpu.make_async_remote_copy(
            src_ref=res.at[:, :, lines, pl.ds((896, 0)[side], 128)],
            dst_ref=xf.at[(0, 9)[side], :, :, lines],
            send_sem=hs.at[2 * h + side], recv_sem=hr.at[2 * h + side],
            device_id=((rng_next, rng_prev)[side], az), device_id_type=MESH,
        )

    def part_copy(t):
        return pltpu.make_async_remote_copy(
            src_ref=sm.at[az], dst_ref=sm.at[az], send_sem=ps.at[t], recv_sem=pr.at[t],
            device_id=(rng, to_az[t]), device_id_type=MESH,
        )

    for t in range(OTHERS):
        part_copy(t).start()
    for h in range(PARTS):

        @pl.when(rng < 15)
        def _(h=h):
            halo_copy(0, h).start()

        @pl.when(rng > 0)
        def _(h=h):
            halo_copy(1, h).start()

    load_chirp.wait()
    lanes = jnp.zeros((1, 128), F32)
    cr_t = toeplitz(jnp.concatenate([cv[0:1, :], lanes], 1), 128).T
    ci_t = toeplitz(jnp.concatenate([cv[1:2, :], lanes], 1), 128).T
    for rows, left, right in ((0, cr_t, -ci_t), (384, ci_t, cr_t)):
        for cols, part in ((0, left), (128, right)):
            high, low = split(part)
            ch[rows : rows + 384, cols : cols + 128] = high
            cl[rows : rows + 384, cols : cols + 128] = low

    for t in range(OTHERS):
        part_copy(t).wait()
    total = sm[0]
    for k in range(1, GROUP):
        total += sm[k]
    sm[GROUP + rng] = total

    def total_copy(t):
        return pltpu.make_async_remote_copy(
            src_ref=sm.at[GROUP + rng], dst_ref=sm.at[GROUP + rng],
            send_sem=qs.at[t], recv_sem=qr.at[t],
            device_id=(to_rng[t], az), device_id_type=MESH,
        )

    for t in range(COLS - 1):
        total_copy(t).start()

    def split_lines(b, h):
        lines = slice(UNIT * h, UNIT * (h + 1))
        for p in range(2):
            for c in range(2):
                high, low = split(xf[b, p, c, lines])
                xh[b, c, h, p * UNIT : (p + 1) * UNIT] = high
                xl[b, c, h, p * UNIT : (p + 1) * UNIT] = low

    def split_block(b, carry):
        for h in range(PARTS):
            split_lines(b, h)
        return carry

    lax.fori_loop(1, 9, split_block, 0)

    for copy in load_img:
        copy.wait()
    lane = lax.broadcasted_iota(jnp.int32, (8, 128), 1)
    pair = lane // 2
    for q in range(4):
        im[q, 0:8] = jnp.zeros((8, 128), F32)
        im[q, 2056:2064] = jnp.zeros((8, 128), F32)

        def pack(k, carry, q=q):
            at = pl.multiple_of(512 * k, 512) + 8
            packed = jnp.zeros((8, 128), F32)
            for g in range(64):
                turned = pltpu.roll(im[q, pl.ds(at + 8 * g, 8), :], 2 * g + 1, 1)
                packed = jnp.where(pair == g, turned, packed)
            pk[4 * q + k] = packed
            return carry

        lax.fori_loop(0, 4, pack, 0)

    def column_copy(side, target):
        return pltpu.make_async_remote_copy(
            src_ref=pk, dst_ref=pc.at[side], send_sem=cs.at[side], recv_sem=cr.at[side],
            device_id=(target // 8, target % 8), device_id_type=MESH,
        )

    cols = [column_copy(0, col_next), column_copy(1, col_prev)]
    for copy in cols:
        copy.start()

    for t in range(COLS - 1):
        total_copy(t).wait()
    total = sm[GROUP]
    for k in range(1, COLS):
        total += sm[GROUP + k]
    total = jnp.sum(total, axis=(0, 1), keepdims=True)
    root_mean = jnp.sqrt(total / (2.0 * 2048 * 16384) + epsilon)
    rm_out[...] = root_mean

    def range_block(j, h, slot):
        high = jnp.concatenate([xh[j + q, c, h] for c in range(2) for q in range(3)], 1)
        low = jnp.concatenate([xl[j + q, c, h] for c in range(2) for q in range(3)], 1)
        result = dot(high, ch[...]) + dot(low, ch[...]) + dot(high, cl[...])
        for p in range(2):
            for c in range(2):
                sb[slot, c * UNIT : (c + 1) * UNIT, p * 128 : (p + 1) * 128] = result[
                    p * UNIT : (p + 1) * UNIT, c * 128 : (c + 1) * 128
                ]

    def turn_copy(h, t):
        dz, dy = 1 - t % 2, t - 3 * (t // 4)
        target = ((zh + dz) % 2) * 4 + (y + dy) % 4
        source = ((zh + dz) % 2) * 4 + (y + 4 - dy) % 4
        slot = OTHERS * h + t
        return target, source, pltpu.make_async_remote_copy(
            src_ref=sb.at[slot], dst_ref=rv.at[slot], send_sem=ss.at[slot], recv_sem=rs.at[slot],
            device_id=(rng, target), device_id_type=MESH,
        )

    for h in range(PARTS):

        @pl.when(rng > 0)
        def _(h=h):
            halo_copy(0, h).wait_recv()

        @pl.when(rng == 0)
        def _(h=h):
            xf[0, :, :, UNIT * h : UNIT * (h + 1)] = jnp.zeros((2, 2, UNIT, 128), F32)

        @pl.when(rng < 15)
        def _(h=h):
            halo_copy(1, h).wait_recv()

        @pl.when(rng == 15)
        def _(h=h):
            xf[9, :, :, UNIT * h : UNIT * (h + 1)] = jnp.zeros((2, 2, UNIT, 128), F32)

        split_lines(0, h)
        split_lines(9, h)

        def send(t, carry, h=h):
            target, _, copy = turn_copy(h, t)
            range_block(target, h, OTHERS * h + t)
            copy.start()
            return carry

        lax.fori_loop(0, OTHERS, send, 0)

    def own(h, carry):
        range_block(az, h, OTHERS * PARTS + h)
        return carry

    lax.fori_loop(0, PARTS, own, 0)

    load_azk.wait()
    lanes = jnp.zeros((1, UNIT), F32)
    factor = -step_size / root_mean
    wr = toeplitz(jnp.concatenate([av[0:1, :] * factor, lanes], 1), UNIT)
    wi = toeplitz(jnp.concatenate([av[1:2, :] * factor, lanes], 1), UNIT)
    for k in range(9):
        e = UNIT * (8 - k)
        part_r, part_i = wr[:, e : e + UNIT], wi[:, e : e + UNIT]
        for c, left, right in ((0, part_r, part_i), (1, -part_i, part_r)):
            rows = slice((2 * k + c) * UNIT, (2 * k + c + 1) * UNIT)
            for at, part in ((0, left), (UNIT, right)):
                high, low = split(part)
                az_mat[rows, at : at + UNIT] = high
                az_mat[rows, at + 2 * UNIT : at + 3 * UNIT] = high
                az_mat[rows, at + 4 * UNIT : at + 5 * UNIT] = low

    for copy in cols:
        copy.wait_recv()
    has_prev = jnp.where(flat > 0, 1.0, 0.0)
    has_next = jnp.where(flat < 127, 1.0, 0.0)
    wide = lax.broadcasted_iota(jnp.int32, (64, 128), 1)
    for q in range(4):

        def regularize(k, carry, q=q):
            at = pl.multiple_of(512 * k, 512)
            edge = jnp.where(
                lane % 2 == 0,
                pltpu.roll(pc[1, 4 * q + k], 127, 1) * has_next,
                pltpu.roll(pc[0, 4 * q + k], 1, 1) * has_prev,
            )
            for h in range(8):
                sides = jnp.concatenate(
                    [pltpu.roll(edge, 127 - 2 * g, 1) for g in range(8 * h, 8 * h + 8)], 0
                )
                v = im[q, pl.ds(at + 64 * h, 80), :]
                mid = v[8:72]
                left = jnp.where(wide == 0, sides, pltpu.roll(mid, 1, 1))
                right = jnp.where(wide == 127, sides, pltpu.roll(mid, 127, 1))
                lap = 4.0 * mid - v[9:73] - v[7:71] - right - left
                out[q // 2, q % 2, pl.ds(at + 64 * h, 64), :] = (
                    mid - (step_size * reg_weight) * lap
                )
            return carry

        lax.fori_loop(0, 4, regularize, 0)

    def azimuth(source, unit):
        high, low = split(source)
        x3[0 : 2 * UNIT] = high
        x3[2 * UNIT : 4 * UNIT] = low
        x3[4 * UNIT : 6 * UNIT] = high
        part = dot(az_mat[...], x3[...])
        for k in range(9):
            v = unit - 4 + k

            @pl.when(jnp.logical_and(v >= 0, v < 2048 // UNIT))
            def _(k=k, v=v):
                lines = pl.ds(pl.multiple_of(UNIT * v, UNIT), UNIT)
                for p in range(2):
                    for c in range(2):
                        at = (2 * k + c) * UNIT
                        out[p, c, lines, :] += part[at : at + UNIT, p * 128 : (p + 1) * 128]

    def own_azimuth(h, carry):
        azimuth(sb[OTHERS * PARTS + h], PARTS * az + h)
        return carry

    lax.fori_loop(0, PARTS, own_azimuth, 0)

    def turn_azimuth(n, carry):
        h, t = n // OTHERS, n % OTHERS
        _, source, copy = turn_copy(h, t)
        copy.wait_recv()
        azimuth(rv[n], PARTS * source + h)
        return carry

    lax.fori_loop(0, PARTS * OTHERS, turn_azimuth, 0)

    for h in range(PARTS):
        for t in range(OTHERS):
            turn_copy(h, t)[2].wait_send()

        @pl.when(rng < 15)
        def _(h=h):
            halo_copy(0, h).wait_send()

        @pl.when(rng > 0)
        def _(h=h):
            halo_copy(1, h).wait_send()

    for copy in cols:
        copy.wait_send()


def local(residual, range_chirp, az_kernel, image_now):
    vmem = pl.BlockSpec(memory_space=pltpu.VMEM)
    hbm = pl.BlockSpec(memory_space=pltpu.HBM)
    dma = pltpu.SemaphoreType.DMA
    turns = PARTS * OTHERS
    image_next, root_mean = pl.pallas_call(
        kernel,
        out_shape=(
            pltpu.VMEM(image_now.shape, F32),
            jax.ShapeDtypeStruct((1, 1), F32),
        ),
        in_specs=[hbm] * 4,
        out_specs=(vmem, vmem),
        scratch_shapes=[
            pltpu.VMEM((10, 2, 2, 256, 128), F32),
            pltpu.VMEM((10, 2, PARTS, 2 * UNIT, 128), BF16),
            pltpu.VMEM((10, 2, PARTS, 2 * UNIT, 128), BF16),
            pltpu.VMEM((2, 256), F32),
            pltpu.VMEM((2, 1024), F32),
            pltpu.VMEM((768, 256), BF16),
            pltpu.VMEM((768, 256), BF16),
            pltpu.VMEM((18 * UNIT, 6 * UNIT), BF16),
            pltpu.VMEM((turns + PARTS, 2 * UNIT, 256), F32),
            pltpu.VMEM((turns, 2 * UNIT, 256), F32),
            pltpu.VMEM((6 * UNIT, 256), BF16),
            pltpu.VMEM((4, 2064, 128), F32),
            pltpu.VMEM((16, 8, 128), F32),
            pltpu.VMEM((2, 16, 8, 128), F32),
            pltpu.VMEM((GROUP + COLS, 8, 128), F32),
            dma((14,)), dma((2 * PARTS,)), dma((2 * PARTS,)), dma((turns,)), dma((turns,)),
            dma((OTHERS,)), dma((OTHERS,)), dma((COLS - 1,)), dma((COLS - 1,)),
            dma((2,)), dma((2,)),
        ],
        compiler_params=pltpu.CompilerParams(
            collective_id=0, has_side_effects=True, vmem_limit_bytes=50 << 20
        ),
        cost_estimate=pl.CostEstimate(
            flops=20_000_000_000, bytes_accessed=12 << 20, transcendentals=0
        ),
        name="sar_step",
    )(residual, range_chirp, az_kernel, image_now)
    return image_next, root_mean.reshape(())


def solution(mesh):
    placed = (
        P(None, None, "az", "rng"),
        P(),
        P(("rng", "az"), None, None),
        P(None, None, None, ("rng", "az")),
    )
    return jax.shard_map(
        local,
        mesh=mesh,
        in_specs=placed,
        out_specs=(P(None, None, None, ("rng", "az")), P()),
        check_vma=False,
    )
```

```python
import jax
import jax.numpy as jnp
from jax import lax
from jax.experimental import pallas as pl
from jax.experimental.pallas import tpu as pltpu
from jax.sharding import PartitionSpec as P

step_size = 0.5
reg_weight = 0.25
epsilon = 1e-06

F32 = jnp.float32
BF16 = jnp.bfloat16
MESH = pl.DeviceIdType.MESH
GROUP = 8
OTHERS = GROUP - 1
COLS = 16
PARTS = 2
LATE = 4
UNIT = 128
TURN = ((0, 1), (1, 0), (2, 1), (3, 0), (1, 1), (2, 0), (3, 1))


def dot(a, b):
    return jnp.dot(a, b, preferred_element_type=F32)


def split(value):
    high = value.astype(BF16)
    return high, (value - high.astype(F32)).astype(BF16)


def toeplitz(row, rows):
    wide = jnp.broadcast_to(row, (rows, row.shape[1]))
    return pltpu.roll(wide, 0, 1, stride=1, stride_axis=0)


def kernel(
    res, chirp, azk, img,
    out, rm_out,
    xf, xh, xl, cv, av, ch, cl, az_mat, sb, rv, x3, im, pk, pc, sm,
    ld, hs, hr, ss, rs, ps, pr, qs, qr, cs, cr, go, ready,
):
    rng, az = lax.axis_index("rng"), lax.axis_index("az")
    zh, y = az // 4, az % 4
    flat = rng * 8 + az
    to_az = [((zh + dz) % 2) * 4 + (y + dy) % 4 for dy, dz in TURN]
    to_rng = [(rng + k) % COLS for k in range(1, COLS)]
    rng_next, rng_prev = (rng + 1) % 16, (rng + 15) % 16
    col_next, col_prev = (flat + 1) % 128, (flat + 127) % 128

    def load_block(b):
        return pltpu.make_async_copy(
            res.at[:, :, :, pl.ds(128 * b, 128)], xf.at[b + 1], ld.at[b]
        )

    load_chirp = pltpu.make_async_copy(chirp, cv, ld.at[8])
    load_azk = pltpu.make_async_copy(azk.at[0], av, ld.at[9])
    load_img = [
        pltpu.make_async_copy(img.at[q // 2, q % 2], im.at[q, pl.ds(8, 2048)], ld.at[10 + q])
        for q in range(4)
    ]
    load_chirp.start()
    for b in range(8):
        load_block(b).start()
    load_azk.start()
    for copy in load_img:
        copy.start()

    barrier = pltpu.get_barrier_semaphore()
    peers = [(rng, target) for target in to_az]
    peers += [(target, az) for target in to_rng]
    peers += [(col_next // 8, col_next % 8), (col_prev // 8, col_prev % 8)]
    for peer in peers:
        pl.semaphore_signal(barrier, inc=1, device_id=peer, device_id_type=MESH)

    load_chirp.wait()
    lanes = jnp.zeros((1, 128), F32)
    cr_t = toeplitz(jnp.concatenate([cv[0:1, :], lanes], 1), 128).T
    ci_t = toeplitz(jnp.concatenate([cv[1:2, :], lanes], 1), 128).T
    for rows, left, right in ((0, cr_t, -ci_t), (384, ci_t, cr_t)):
        for cols, part in ((0, left), (128, right)):
            high, low = split(part)
            ch[rows : rows + 384, cols : cols + 128] = high
            cl[rows : rows + 384, cols : cols + 128] = low

    for b in range(8):
        load_block(b).wait()

    def squares(b, total):
        for p in range(2):
            for c in range(2):
                v = xf[b, p, c]
                total += jnp.sum((v * v).reshape(32, 8, 128), axis=0)
        return total

    sm[az] = lax.fori_loop(1, 9, squares, jnp.zeros((8, 128), F32))

    pl.semaphore_wait(barrier, len(peers))

    def halo_copy(side, h):
        lines = pl.ds(UNIT * h, UNIT)
        return pltpu.make_async_remote_copy(
            src_ref=res.at[:, :, lines, pl.ds((896, 0)[side], 128)],
            dst_ref=xf.at[(0, 9)[side], :, :, lines],
            send_sem=hs.at[2 * h + side], recv_sem=hr.at[2 * h + side],
            device_id=((rng_next, rng_prev)[side], az), device_id_type=MESH,
        )

    def part_copy(t):
        return pltpu.make_async_remote_copy(
            src_ref=sm.at[az], dst_ref=sm.at[az], send_sem=ps.at[t], recv_sem=pr.at[t],
            device_id=(rng, to_az[t]), device_id_type=MESH,
        )

    for t in range(OTHERS):
        part_copy(t).start()
    for h in range(PARTS):

        @pl.when(rng < 15)
        def _(h=h):
            halo_copy(0, h).start()

        @pl.when(rng > 0)
        def _(h=h):
            halo_copy(1, h).start()

    def split_lines(b, h):
        lines = slice(UNIT * h, UNIT * (h + 1))
        for p in range(2):
            for c in range(2):
                high, low = split(xf[b, p, c, lines])
                xh[b, c, h, p * UNIT : (p + 1) * UNIT] = high
                xl[b, c, h, p * UNIT : (p + 1) * UNIT] = low

    def split_part(h):
        def body(b, carry):
            split_lines(b, h)
            return carry

        lax.fori_loop(1, 9, body, 0)

    split_part(0)

    for t in range(OTHERS):
        part_copy(t).wait()
    total = sm[0]
    for k in range(1, GROUP):
        total += sm[k]
    sm[GROUP + rng] = total

    def total_copy(t):
        return pltpu.make_async_remote_copy(
            src_ref=sm.at[GROUP + rng], dst_ref=sm.at[GROUP + rng],
            send_sem=qs.at[t], recv_sem=qr.at[t],
            device_id=(to_rng[t], az), device_id_type=MESH,
        )

    for t in range(COLS - 1):
        total_copy(t).start()

    def range_block(j, h, slot):
        high = jnp.concatenate([xh[j + q, c, h] for c in range(2) for q in range(3)], 1)
        low = jnp.concatenate([xl[j + q, c, h] for c in range(2) for q in range(3)], 1)
        result = dot(high, ch[...]) + dot(low, ch[...]) + dot(high, cl[...])
        for p in range(2):
            for c in range(2):
                sb[slot, c * UNIT : (c + 1) * UNIT, p * 128 : (p + 1) * 128] = result[
                    p * UNIT : (p + 1) * UNIT, c * 128 : (c + 1) * 128
                ]

    def turn_copy(h, t):
        dz, dy = 1 - t % 2, t - 3 * (t // 4)
        target = ((zh + dz) % 2) * 4 + (y + dy) % 4
        source = ((zh + dz) % 2) * 4 + (y + 4 - dy) % 4
        slot = OTHERS * h + t
        return target, source, pltpu.make_async_remote_copy(
            src_ref=sb.at[slot], dst_ref=rv.at[slot], send_sem=ss.at[slot], recv_sem=rs.at[slot],
            device_id=(rng, target), device_id_type=MESH,
        )

    def send_part(h):

        @pl.when(rng > 0)
        def _():
            halo_copy(0, h).wait_recv()

        @pl.when(rng == 0)
        def _():
            xf[0, :, :, UNIT * h : UNIT * (h + 1)] = jnp.zeros((2, 2, UNIT, 128), F32)

        @pl.when(rng < 15)
        def _():
            halo_copy(1, h).wait_recv()

        @pl.when(rng == 15)
        def _():
            xf[9, :, :, UNIT * h : UNIT * (h + 1)] = jnp.zeros((2, 2, UNIT, 128), F32)

        if h == 0:
            for near, end in ((1, 0), (COLS - 2, COLS - 1)):

                @pl.when(rng == near)
                def _():
                    pl.semaphore_signal(go, inc=1, device_id=(end, az), device_id_type=MESH)

                @pl.when(rng == end)
                def _():
                    pl.semaphore_wait(go, 1)

        if h == 0:
            for target in to_az:
                pl.semaphore_signal(ready, inc=1, device_id=(rng, target), device_id_type=MESH)
            pl.semaphore_wait(ready, OTHERS)
        split_lines(0, h)
        split_lines(9, h)

        def send(t, carry):
            target, _, copy = turn_copy(h, t)
            range_block(target, h, OTHERS * h + t)
            copy.start()
            return carry

        lax.fori_loop(0, OTHERS, send, 0)

    send_part(0)

    for copy in load_img:
        copy.wait()
    lane = lax.broadcasted_iota(jnp.int32, (8, 128), 1)
    for q in range(4):
        im[q, 0:8] = jnp.zeros((8, 128), F32)
        im[q, 2056:2064] = jnp.zeros((8, 128), F32)

        def pack(k, carry, q=q):
            at = pl.multiple_of(1024 * k, 1024) + 8
            head = tail = jnp.zeros((8, 128), F32)
            for g in range(128):
                turned = pltpu.roll(im[q, pl.ds(at + 8 * g, 8), :], g, 1)
                head = jnp.where(lane == g, turned, head)
                tail = jnp.where(lane == (g + 127) % 128, turned, tail)
            pk[0, 2 * q + k] = tail
            pk[1, 2 * q + k] = head
            return carry

        lax.fori_loop(0, 2, pack, 0)

    def column_copy(side, target):
        return pltpu.make_async_remote_copy(
            src_ref=pk.at[side], dst_ref=pc.at[side], send_sem=cs.at[side], recv_sem=cr.at[side],
            device_id=(target // 8, target % 8), device_id_type=MESH,
        )

    cols = [column_copy(0, col_next), column_copy(1, col_prev)]
    for copy in cols:
        copy.start()

    split_part(1)
    send_part(1)

    def own(h, carry):
        range_block(az, h, OTHERS * PARTS + h)
        return carry

    lax.fori_loop(0, PARTS, own, 0)

    for t in range(COLS - 1):
        total_copy(t).wait()
    total = sm[GROUP]
    for k in range(1, COLS):
        total += sm[GROUP + k]
    total = jnp.sum(total, axis=(0, 1), keepdims=True)
    root_mean = jnp.sqrt(total / (2.0 * 2048 * 16384) + epsilon)
    rm_out[...] = root_mean

    load_azk.wait()
    lanes = jnp.zeros((1, UNIT), F32)
    factor = -step_size / root_mean
    wr = toeplitz(jnp.concatenate([av[0:1, :] * factor, lanes], 1), UNIT)
    wi = toeplitz(jnp.concatenate([av[1:2, :] * factor, lanes], 1), UNIT)
    for k in range(9):
        e = UNIT * (8 - k)
        part_r, part_i = wr[:, e : e + UNIT], wi[:, e : e + UNIT]
        for c, left, right in ((0, part_r, part_i), (1, -part_i, part_r)):
            rows = slice((2 * k + c) * UNIT, (2 * k + c + 1) * UNIT)
            for at, part in ((0, left), (UNIT, right)):
                high, low = split(part)
                az_mat[rows, at : at + UNIT] = high
                az_mat[rows, at + 2 * UNIT : at + 3 * UNIT] = high
                az_mat[rows, at + 4 * UNIT : at + 5 * UNIT] = low

    def azimuth(source, unit):
        high, low = split(source)
        x3[0 : 2 * UNIT] = high
        x3[2 * UNIT : 4 * UNIT] = low
        x3[4 * UNIT : 6 * UNIT] = high
        part = dot(az_mat[...], x3[...])
        for k in range(9):
            v = unit - 4 + k

            @pl.when(jnp.logical_and(v >= 0, v < 2048 // UNIT))
            def _(k=k, v=v):
                lines = pl.ds(pl.multiple_of(UNIT * v, UNIT), UNIT)
                for p in range(2):
                    for c in range(2):
                        at = (2 * k + c) * UNIT
                        out[p, c, lines, :] += part[at : at + UNIT, p * 128 : (p + 1) * 128]

    out[...] = jnp.zeros_like(out)

    def own_azimuth(h, carry):
        azimuth(sb[OTHERS * PARTS + h], PARTS * az + h)
        return carry

    lax.fori_loop(0, PARTS, own_azimuth, 0)

    def turn_azimuth(n, carry):
        h, t = n // OTHERS, n % OTHERS
        _, source, copy = turn_copy(h, t)
        copy.wait_recv()
        azimuth(rv[n], PARTS * source + h)
        return carry

    lax.fori_loop(0, LATE, turn_azimuth, 0)

    for copy in cols:
        copy.wait_recv()
    has_prev = jnp.where(flat > 0, 1.0, 0.0)
    has_next = jnp.where(flat < 127, 1.0, 0.0)
    wide = lax.broadcasted_iota(jnp.int32, (64, 128), 1)
    for q in range(4):

        def regularize(k, carry, q=q):
            at = pl.multiple_of(512 * k, 512)
            before = pc[0, 2 * q + k // 2] * has_prev
            after = pc[1, 2 * q + k // 2] * has_next
            before = jnp.where(k % 2 == 1, pltpu.roll(before, 64, 1), before)
            after = jnp.where(k % 2 == 1, pltpu.roll(after, 64, 1), after)
            for h in range(8):
                rows = range(8 * h, 8 * h + 8)
                lefts = jnp.concatenate([pltpu.roll(before, (129 - g) % 128, 1) for g in rows], 0)
                rights = jnp.concatenate([pltpu.roll(after, 127 - g, 1) for g in rows], 0)
                v = im[q, pl.ds(at + 64 * h, 80), :]
                mid = v[8:72]
                left = jnp.where(wide == 0, lefts, pltpu.roll(mid, 1, 1))
                right = jnp.where(wide == 127, rights, pltpu.roll(mid, 127, 1))
                lap = 4.0 * mid - v[9:73] - v[7:71] - right - left
                out[q // 2, q % 2, pl.ds(at + 64 * h, 64), :] += (
                    mid - (step_size * reg_weight) * lap
                )
            return carry

        lax.fori_loop(0, 4, regularize, 0)

    lax.fori_loop(LATE, PARTS * OTHERS, turn_azimuth, 0)

    for h in range(PARTS):
        for t in range(OTHERS):
            turn_copy(h, t)[2].wait_send()

        @pl.when(rng < 15)
        def _(h=h):
            halo_copy(0, h).wait_send()

        @pl.when(rng > 0)
        def _(h=h):
            halo_copy(1, h).wait_send()

    for copy in cols:
        copy.wait_send()


def local(residual, range_chirp, az_kernel, image_now):
    vmem = pl.BlockSpec(memory_space=pltpu.VMEM)
    hbm = pl.BlockSpec(memory_space=pltpu.HBM)
    dma = pltpu.SemaphoreType.DMA
    turns = PARTS * OTHERS
    image_next, root_mean = pl.pallas_call(
        kernel,
        out_shape=(
            pltpu.VMEM(image_now.shape, F32),
            jax.ShapeDtypeStruct((1, 1), F32),
        ),
        in_specs=[hbm] * 4,
        out_specs=(vmem, vmem),
        scratch_shapes=[
            pltpu.VMEM((10, 2, 2, 256, 128), F32),
            pltpu.VMEM((10, 2, PARTS, 2 * UNIT, 128), BF16),
            pltpu.VMEM((10, 2, PARTS, 2 * UNIT, 128), BF16),
            pltpu.VMEM((2, 256), F32),
            pltpu.VMEM((2, 1024), F32),
            pltpu.VMEM((768, 256), BF16),
            pltpu.VMEM((768, 256), BF16),
            pltpu.VMEM((18 * UNIT, 6 * UNIT), BF16),
            pltpu.VMEM((turns + PARTS, 2 * UNIT, 256), F32),
            pltpu.VMEM((turns, 2 * UNIT, 256), F32),
            pltpu.VMEM((6 * UNIT, 256), BF16),
            pltpu.VMEM((4, 2064, 128), F32),
            pltpu.VMEM((2, 8, 8, 128), F32),
            pltpu.VMEM((2, 8, 8, 128), F32),
            pltpu.VMEM((GROUP + COLS, 8, 128), F32),
            dma((14,)), dma((2 * PARTS,)), dma((2 * PARTS,)), dma((turns,)), dma((turns,)),
            dma((OTHERS,)), dma((OTHERS,)), dma((COLS - 1,)), dma((COLS - 1,)),
            dma((2,)), dma((2,)), pltpu.SemaphoreType.REGULAR, pltpu.SemaphoreType.REGULAR,
        ],
        compiler_params=pltpu.CompilerParams(
            collective_id=0, has_side_effects=True, vmem_limit_bytes=50 << 20
        ),
        cost_estimate=pl.CostEstimate(
            flops=20_000_000_000, bytes_accessed=12 << 20, transcendentals=0
        ),
        name="sar_step",
    )(residual, range_chirp, az_kernel, image_now)
    return image_next, root_mean.reshape(())


def solution(mesh):
    placed = (
        P(None, None, "az", "rng"),
        P(),
        P(("rng", "az"), None, None),
        P(None, None, None, ("rng", "az")),
    )
    return jax.shard_map(
        local,
        mesh=mesh,
        in_specs=placed,
        out_specs=(P(None, None, None, ("rng", "az")), P()),
        check_vma=False,
    )
```

```python
import jax
import jax.numpy as jnp
from jax import lax
from jax.experimental import pallas as pl
from jax.experimental.pallas import tpu as pltpu
from jax.sharding import PartitionSpec as P

step_size = 0.5
reg_weight = 0.25
epsilon = 1e-06

F32 = jnp.float32
BF16 = jnp.bfloat16
MESH = pl.DeviceIdType.MESH
GROUP = 8
OTHERS = GROUP - 1
COLS = 16
PARTS = 2
LATE = 2
UNIT = 128
TURN = ((0, 1), (1, 0), (2, 1), (3, 0), (1, 1), (2, 0), (3, 1))


def dot(a, b):
    return jnp.dot(a, b, preferred_element_type=F32)


def split(value):
    high = value.astype(BF16)
    return high, (value - high.astype(F32)).astype(BF16)


def toeplitz(row, rows):
    wide = jnp.broadcast_to(row, (rows, row.shape[1]))
    return pltpu.roll(wide, 0, 1, stride=1, stride_axis=0)


def kernel(
    res, chirp, azk, img,
    out, rm_out,
    xf, xh, xl, cv, av, ch, cl, az_mat, sb, rv, x3, im, pk, pc, sm,
    ld, hs, hr, ss, rs, ps, pr, qs, qr, cs, cr, go, ready,
):
    rng, az = lax.axis_index("rng"), lax.axis_index("az")
    zh, y = az // 4, az % 4
    flat = rng * 8 + az
    to_az = [((zh + dz) % 2) * 4 + (y + dy) % 4 for dy, dz in TURN]
    to_rng = [(rng + k) % COLS for k in range(1, COLS)]
    rng_next, rng_prev = (rng + 1) % 16, (rng + 15) % 16
    col_next, col_prev = (flat + 1) % 128, (flat + 127) % 128

    def load_block(b):
        return pltpu.make_async_copy(
            res.at[:, :, :, pl.ds(128 * b, 128)], xf.at[b + 1], ld.at[b]
        )

    load_chirp = pltpu.make_async_copy(chirp, cv, ld.at[8])
    load_azk = pltpu.make_async_copy(azk.at[0], av, ld.at[9])
    load_img = [
        pltpu.make_async_copy(img.at[q // 2, q % 2], im.at[q, pl.ds(8, 2048)], ld.at[10 + q])
        for q in range(4)
    ]
    load_chirp.start()
    for b in range(8):
        load_block(b).start()
    load_azk.start()
    for copy in load_img:
        copy.start()

    barrier = pltpu.get_barrier_semaphore()
    peers = [(rng, target) for target in to_az]
    peers += [(target, az) for target in to_rng]
    peers += [(col_next // 8, col_next % 8), (col_prev // 8, col_prev % 8)]
    for peer in peers:
        pl.semaphore_signal(barrier, inc=1, device_id=peer, device_id_type=MESH)

    load_chirp.wait()
    lanes = jnp.zeros((1, 128), F32)
    cr_t = toeplitz(jnp.concatenate([cv[0:1, :], lanes], 1), 128).T
    ci_t = toeplitz(jnp.concatenate([cv[1:2, :], lanes], 1), 128).T
    for rows, left, right in ((0, cr_t, -ci_t), (384, ci_t, cr_t)):
        for cols, part in ((0, left), (128, right)):
            high, low = split(part)
            ch[rows : rows + 384, cols : cols + 128] = high
            cl[rows : rows + 384, cols : cols + 128] = low

    for b in range(8):
        load_block(b).wait()

    def squares(b, total):
        for p in range(2):
            for c in range(2):
                v = xf[b, p, c]
                total += jnp.sum((v * v).reshape(32, 8, 128), axis=0)
        return total

    sm[az] = lax.fori_loop(1, 9, squares, jnp.zeros((8, 128), F32))

    pl.semaphore_wait(barrier, len(peers))

    def halo_copy(side, h):
        lines = pl.ds(UNIT * h, UNIT)
        return pltpu.make_async_remote_copy(
            src_ref=res.at[:, :, lines, pl.ds((896, 0)[side], 128)],
            dst_ref=xf.at[(0, 9)[side], :, :, lines],
            send_sem=hs.at[2 * h + side], recv_sem=hr.at[2 * h + side],
            device_id=((rng_next, rng_prev)[side], az), device_id_type=MESH,
        )

    def part_copy(t):
        return pltpu.make_async_remote_copy(
            src_ref=sm.at[az], dst_ref=sm.at[az], send_sem=ps.at[t], recv_sem=pr.at[t],
            device_id=(rng, to_az[t]), device_id_type=MESH,
        )

    for t in range(OTHERS):
        part_copy(t).start()
    for h in range(PARTS):

        @pl.when(rng < 15)
        def _(h=h):
            halo_copy(0, h).start()

        @pl.when(rng > 0)
        def _(h=h):
            halo_copy(1, h).start()

    def split_lines(b, h):
        lines = slice(UNIT * h, UNIT * (h + 1))
        for p in range(2):
            for c in range(2):
                high, low = split(xf[b, p, c, lines])
                xh[b, c, h, p * UNIT : (p + 1) * UNIT] = high
                xl[b, c, h, p * UNIT : (p + 1) * UNIT] = low

    def split_part(h):
        def body(b, carry):
            split_lines(b, h)
            return carry

        lax.fori_loop(1, 9, body, 0)

    split_part(0)

    for t in range(OTHERS):
        part_copy(t).wait()
    total = sm[0]
    for k in range(1, GROUP):
        total += sm[k]
    sm[GROUP + rng] = total

    def total_copy(t):
        return pltpu.make_async_remote_copy(
            src_ref=sm.at[GROUP + rng], dst_ref=sm.at[GROUP + rng],
            send_sem=qs.at[t], recv_sem=qr.at[t],
            device_id=(to_rng[t], az), device_id_type=MESH,
        )

    for t in range(COLS - 1):
        total_copy(t).start()

    def range_block(j, h, slot):
        high = jnp.concatenate([xh[j + q, c, h] for c in range(2) for q in range(3)], 1)
        low = jnp.concatenate([xl[j + q, c, h] for c in range(2) for q in range(3)], 1)
        result = dot(high, ch[...]) + dot(low, ch[...]) + dot(high, cl[...])
        for p in range(2):
            for c in range(2):
                sb[slot, c * UNIT : (c + 1) * UNIT, p * 128 : (p + 1) * 128] = result[
                    p * UNIT : (p + 1) * UNIT, c * 128 : (c + 1) * 128
                ]

    def turn_copy(h, t):
        dz, dy = 1 - t % 2, t - 3 * (t // 4)
        target = ((zh + dz) % 2) * 4 + (y + dy) % 4
        source = ((zh + dz) % 2) * 4 + (y + 4 - dy) % 4
        slot = OTHERS * h + t
        return target, source, pltpu.make_async_remote_copy(
            src_ref=sb.at[slot], dst_ref=rv.at[slot], send_sem=ss.at[slot], recv_sem=rs.at[slot],
            device_id=(rng, target), device_id_type=MESH,
        )

    def send_part(h):

        @pl.when(rng > 0)
        def _():
            halo_copy(0, h).wait_recv()

        @pl.when(rng == 0)
        def _():
            xf[0, :, :, UNIT * h : UNIT * (h + 1)] = jnp.zeros((2, 2, UNIT, 128), F32)

        @pl.when(rng < 15)
        def _():
            halo_copy(1, h).wait_recv()

        @pl.when(rng == 15)
        def _():
            xf[9, :, :, UNIT * h : UNIT * (h + 1)] = jnp.zeros((2, 2, UNIT, 128), F32)

        if h == 0:
            for near, end in ((1, 0), (COLS - 2, COLS - 1)):

                @pl.when(rng == near)
                def _():
                    pl.semaphore_signal(go, inc=1, device_id=(end, az), device_id_type=MESH)

                @pl.when(rng == end)
                def _():
                    pl.semaphore_wait(go, 1)

        if h == 0:
            for target in to_az:
                pl.semaphore_signal(ready, inc=1, device_id=(rng, target), device_id_type=MESH)
            pl.semaphore_wait(ready, OTHERS)
        split_lines(0, h)
        split_lines(9, h)

        def send(t, carry):
            target, _, copy = turn_copy(h, t)
            range_block(target, h, OTHERS * h + t)
            copy.start()
            return carry

        lax.fori_loop(0, OTHERS, send, 0)

    send_part(0)

    for copy in load_img:
        copy.wait()
    lane = lax.broadcasted_iota(jnp.int32, (8, 128), 1)
    for q in range(4):
        im[q, 0:8] = jnp.zeros((8, 128), F32)
        im[q, 2056:2064] = jnp.zeros((8, 128), F32)

        def pack(k, carry, q=q):
            at = pl.multiple_of(1024 * k, 1024) + 8
            head = tail = jnp.zeros((8, 128), F32)
            for g in range(128):
                turned = pltpu.roll(im[q, pl.ds(at + 8 * g, 8), :], g, 1)
                head = jnp.where(lane == g, turned, head)
                tail = jnp.where(lane == (g + 127) % 128, turned, tail)
            pk[0, 2 * q + k] = tail
            pk[1, 2 * q + k] = head
            return carry

        lax.fori_loop(0, 2, pack, 0)

    def column_copy(side, target):
        return pltpu.make_async_remote_copy(
            src_ref=pk.at[side], dst_ref=pc.at[side], send_sem=cs.at[side], recv_sem=cr.at[side],
            device_id=(target // 8, target % 8), device_id_type=MESH,
        )

    cols = [column_copy(0, col_next), column_copy(1, col_prev)]
    for copy in cols:
        copy.start()

    split_part(1)
    send_part(1)

    def own(h, carry):
        range_block(az, h, OTHERS * PARTS + h)
        return carry

    lax.fori_loop(0, PARTS, own, 0)

    for t in range(COLS - 1):
        total_copy(t).wait()
    total = sm[GROUP]
    for k in range(1, COLS):
        total += sm[GROUP + k]
    total = jnp.sum(total, axis=(0, 1), keepdims=True)
    root_mean = jnp.sqrt(total / (2.0 * 2048 * 16384) + epsilon)
    rm_out[...] = root_mean

    load_azk.wait()
    lanes = jnp.zeros((1, UNIT), F32)
    factor = -step_size / root_mean
    wr = toeplitz(jnp.concatenate([av[0:1, :] * factor, lanes], 1), UNIT)
    wi = toeplitz(jnp.concatenate([av[1:2, :] * factor, lanes], 1), UNIT)
    for k in range(9):
        e = UNIT * (8 - k)
        part_r, part_i = wr[:, e : e + UNIT], wi[:, e : e + UNIT]
        for c, left, right in ((0, part_r, part_i), (1, -part_i, part_r)):
            rows = slice((2 * k + c) * UNIT, (2 * k + c + 1) * UNIT)
            for at, part in ((0, left), (UNIT, right)):
                high, low = split(part)
                az_mat[rows, at : at + UNIT] = high
                az_mat[rows, at + 2 * UNIT : at + 3 * UNIT] = high
                az_mat[rows, at + 4 * UNIT : at + 5 * UNIT] = low

    def azimuth(source, unit):
        high, low = split(source)
        x3[0 : 2 * UNIT] = high
        x3[2 * UNIT : 4 * UNIT] = low
        x3[4 * UNIT : 6 * UNIT] = high
        part = dot(az_mat[...], x3[...])
        for k in range(9):
            v = unit - 4 + k

            @pl.when(jnp.logical_and(v >= 0, v < 2048 // UNIT))
            def _(k=k, v=v):
                lines = pl.ds(pl.multiple_of(UNIT * v, UNIT), UNIT)
                for p in range(2):
                    for c in range(2):
                        at = (2 * k + c) * UNIT
                        out[p, c, lines, :] += part[at : at + UNIT, p * 128 : (p + 1) * 128]

    out[...] = jnp.zeros_like(out)

    def own_azimuth(h, carry):
        azimuth(sb[OTHERS * PARTS + h], PARTS * az + h)
        return carry

    lax.fori_loop(0, PARTS, own_azimuth, 0)

    def turn_azimuth(n, carry):
        h, t = n // OTHERS, n % OTHERS
        _, source, copy = turn_copy(h, t)
        copy.wait_recv()
        azimuth(rv[n], PARTS * source + h)
        return carry

    lax.fori_loop(0, LATE, turn_azimuth, 0)

    for copy in cols:
        copy.wait_recv()
    has_prev = jnp.where(flat > 0, 1.0, 0.0)
    has_next = jnp.where(flat < 127, 1.0, 0.0)
    wide = lax.broadcasted_iota(jnp.int32, (64, 128), 1)
    for q in range(4):

        def regularize(k, carry, q=q):
            at = pl.multiple_of(512 * k, 512)
            before = pc[0, 2 * q + k // 2] * has_prev
            after = pc[1, 2 * q + k // 2] * has_next
            before = jnp.where(k % 2 == 1, pltpu.roll(before, 64, 1), before)
            after = jnp.where(k % 2 == 1, pltpu.roll(after, 64, 1), after)
            for h in range(8):
                rows = range(8 * h, 8 * h + 8)
                lefts = jnp.concatenate([pltpu.roll(before, (129 - g) % 128, 1) for g in rows], 0)
                rights = jnp.concatenate([pltpu.roll(after, 127 - g, 1) for g in rows], 0)
                v = im[q, pl.ds(at + 64 * h, 80), :]
                mid = v[8:72]
                left = jnp.where(wide == 0, lefts, pltpu.roll(mid, 1, 1))
                right = jnp.where(wide == 127, rights, pltpu.roll(mid, 127, 1))
                lap = 4.0 * mid - v[9:73] - v[7:71] - right - left
                out[q // 2, q % 2, pl.ds(at + 64 * h, 64), :] += (
                    mid - (step_size * reg_weight) * lap
                )
            return carry

        lax.fori_loop(0, 4, regularize, 0)

    lax.fori_loop(LATE, PARTS * OTHERS, turn_azimuth, 0)

    for h in range(PARTS):
        for t in range(OTHERS):
            turn_copy(h, t)[2].wait_send()

        @pl.when(rng < 15)
        def _(h=h):
            halo_copy(0, h).wait_send()

        @pl.when(rng > 0)
        def _(h=h):
            halo_copy(1, h).wait_send()

    for copy in cols:
        copy.wait_send()


def local(residual, range_chirp, az_kernel, image_now):
    vmem = pl.BlockSpec(memory_space=pltpu.VMEM)
    hbm = pl.BlockSpec(memory_space=pltpu.HBM)
    dma = pltpu.SemaphoreType.DMA
    turns = PARTS * OTHERS
    image_next, root_mean = pl.pallas_call(
        kernel,
        out_shape=(
            pltpu.VMEM(image_now.shape, F32),
            jax.ShapeDtypeStruct((1, 1), F32),
        ),
        in_specs=[hbm] * 4,
        out_specs=(vmem, vmem),
        scratch_shapes=[
            pltpu.VMEM((10, 2, 2, 256, 128), F32),
            pltpu.VMEM((10, 2, PARTS, 2 * UNIT, 128), BF16),
            pltpu.VMEM((10, 2, PARTS, 2 * UNIT, 128), BF16),
            pltpu.VMEM((2, 256), F32),
            pltpu.VMEM((2, 1024), F32),
            pltpu.VMEM((768, 256), BF16),
            pltpu.VMEM((768, 256), BF16),
            pltpu.VMEM((18 * UNIT, 6 * UNIT), BF16),
            pltpu.VMEM((turns + PARTS, 2 * UNIT, 256), F32),
            pltpu.VMEM((turns, 2 * UNIT, 256), F32),
            pltpu.VMEM((6 * UNIT, 256), BF16),
            pltpu.VMEM((4, 2064, 128), F32),
            pltpu.VMEM((2, 8, 8, 128), F32),
            pltpu.VMEM((2, 8, 8, 128), F32),
            pltpu.VMEM((GROUP + COLS, 8, 128), F32),
            dma((14,)), dma((2 * PARTS,)), dma((2 * PARTS,)), dma((turns,)), dma((turns,)),
            dma((OTHERS,)), dma((OTHERS,)), dma((COLS - 1,)), dma((COLS - 1,)),
            dma((2,)), dma((2,)), pltpu.SemaphoreType.REGULAR, pltpu.SemaphoreType.REGULAR,
        ],
        compiler_params=pltpu.CompilerParams(
            collective_id=0, has_side_effects=True, vmem_limit_bytes=50 << 20
        ),
        cost_estimate=pl.CostEstimate(
            flops=20_000_000_000, bytes_accessed=12 << 20, transcendentals=0
        ),
        name="sar_step",
    )(residual, range_chirp, az_kernel, image_now)
    return image_next, root_mean.reshape(())


def solution(mesh):
    placed = (
        P(None, None, "az", "rng"),
        P(),
        P(("rng", "az"), None, None),
        P(None, None, None, ("rng", "az")),
    )
    return jax.shard_map(
        local,
        mesh=mesh,
        in_specs=placed,
        out_specs=(P(None, None, None, ("rng", "az")), P()),
        check_vma=False,
    )
```
